256 devices in a mesh: row: 8 (over z), col: 32 (over y, x, core).
Axes of the slice: x: 4, y: 4, z: 8, core: 2. Of those that a mesh axis runs over, the one named last changes fastest.
Arguments:
- left_blocks: bfloat16 [8, 32, 32, 128, 128], P('row', 'col'), may hold values from -6 to 6
- left_cols: int32 [8, 32, 32], P(None, 'col'), may hold values from 0 to 63, as said below
- reach_blocks: bfloat16 [64, 32, 128, 128], P('row', 'col'), may hold values from -0.125 to 0.125
- reach_cols: int32 [64, 32], P('row'), may hold values from 0 to 63, all different within a row
Outputs:
- product: bfloat16 [8, 32, 32, 128, 128], P('row', 'col')
The draws below stay inside these ranges and needn't reach their ends.
Inputs may be any that keep to these rules, and one draw needn't show every extreme that they name: `left_cols`: within each slab row the 32 block columns are distinct; at most 8 of them lie in one panel of 8 block columns (panel q holds columns q * 8 to (q + 1) * 8 - 1), and every row has exactly 8 in some panel. `reach_cols`: within each reached block row the 32 block columns are distinct.
All inputs are finite; a program needn't handle non-finite values.
Results may differ from the reference program's by a relative error of at most 0.017.
Values may be sent and summed in bfloat16 or wider, within the bound.
No kernel may reach another device: no remote copies, remote signals or barrier semaphores. Data moves between devices by JAX's collectives and lax.ppermute only.
A program may use at most 192 MiB of HBM per device.

```python
import jax
import jax.numpy as jnp
from jax import lax

BLK = 128
KEPT = 32
CAP = 8
PAN_ROWS = 8
SLAB_PAN = 32
REACH = 64
N_ROW = 8


def draw_left_cols(key, part):
    key = jax.random.fold_in(key, 11)
    key_order, key_home, key_pick = jax.random.split(key, 3)
    total_rows = N_ROW * SLAB_PAN
    order_draw = jax.random.randint(key_order, (total_rows, N_ROW, PAN_ROWS), 0, 1 << 20)
    order_score = order_draw * PAN_ROWS + jnp.arange(PAN_ROWS, dtype=jnp.int32)[None, None, :]
    local_cols = jnp.argsort(order_score, axis=2, stable=True)[:, :, :CAP].astype(jnp.int32)
    panel_ids = jnp.arange(N_ROW, dtype=jnp.int32)
    candidates = local_cols + (panel_ids * PAN_ROWS)[None, :, None]
    home = jax.random.randint(key_home, (total_rows, 1, 1), 0, N_ROW)
    apart = jnp.abs(panel_ids[None, :, None] - home)
    apart = jnp.minimum(apart, N_ROW - apart)
    pick_draw = jax.random.randint(key_pick, (total_rows, N_ROW, CAP), 0, 1 << 16)
    priority = jnp.where(apart == 0, 1 << 22, pick_draw - apart * (1 << 14))
    flat_priority = priority.reshape((total_rows, N_ROW * CAP)) * (N_ROW * CAP) + jnp.arange(N_ROW * CAP, dtype=jnp.int32)[None, :]
    chosen = lax.top_k(flat_priority, KEPT)[1]
    flat_cand = candidates.reshape((total_rows, N_ROW * CAP))
    picked_cols = jnp.take_along_axis(flat_cand, chosen, axis=1)
    return picked_cols.reshape((N_ROW, SLAB_PAN, KEPT)).astype(jnp.int32)


def block_scale(key, extent, shards, least, high):
    level = 1.0
    for dim, parts in shards:
        draws = jax.random.uniform(jax.random.fold_in(jax.random.fold_in(key, 6), dim), (parts,), jnp.float32, least / len(shards), high / len(shards))
        level = level * jnp.repeat(jnp.exp(draws), extent[dim] // parts).reshape((-1,) + (1,) * (len(extent) - 1 - dim))
    return level


def choose_distinct(key, rows, amount, top, lift):
    order = jax.random.permutation(jax.random.fold_in(key, 1), amount)
    pull = order
    for power in range(3):
        pull = pull * pull // amount
    pull = pull * lift // amount
    tickets = jax.random.randint(jax.random.fold_in(key, 2), (rows, amount), 0, 4096) + pull
    sure = jax.random.permutation(jax.random.fold_in(key, 3), rows)[jnp.arange(amount) % rows]
    tickets = jnp.where(jnp.arange(rows)[:, None] == sure[None, :], 1 << 14, tickets)
    score = tickets * amount + jnp.arange(amount)
    return lax.top_k(score.astype(jnp.int32), top)[1].astype(jnp.int32)


def gaussian(rng, dims, spread, limit, cuts=(), kind=jnp.bfloat16):
    entries = jax.random.normal(rng, dims, jnp.float32) * spread
    if len(cuts) > 0:
        entries = block_scale(rng, dims, cuts, -0.22, 0.18) * entries
    return jnp.clip(entries, min=-limit, max=limit).astype(kind)


def setup_inputs(seed: int = 0) -> dict:
    key_list = jax.random.split(jax.random.key(seed), 5)
    left_blocks = gaussian(key_list[0], (N_ROW, SLAB_PAN, KEPT, BLK, BLK), 1.0, 6.0, ((0, 8), (1, 32)))
    left_cols = draw_left_cols(jax.random.fold_in(key_list[4], 71), 0)
    reach_blocks = gaussian(key_list[2], (REACH, KEPT, BLK, BLK), (BLK * KEPT * KEPT // REACH) ** -0.5, 0.125, ((0, 8), (1, 32)))
    reach_cols = choose_distinct(key_list[3], REACH, REACH, KEPT, 0)
    return dict(left_blocks=left_blocks, left_cols=left_cols, reach_blocks=reach_blocks, reach_cols=reach_cols)


def slab_row(blocks, cols_row, reach_blocks, reach_cols):
    slots = cols_row.shape[0]
    reach_row = reach_cols[cols_row]
    matches = reach_row[:, None, :] == cols_row[None, :, None]
    present = jnp.any(matches, axis=2)
    slot_pick = jnp.sum(jnp.where(matches, jnp.arange(slots, dtype=jnp.int32)[None, None, :], 0), axis=2).astype(jnp.int32)
    chosen = reach_blocks[cols_row[:, None], slot_pick]
    chosen = jnp.where(present[:, :, None, None], chosen, jnp.zeros((), chosen.dtype))
    pieces = jnp.einsum('axy,asyz->asxz', blocks.astype(jnp.float32), chosen.astype(jnp.float32), precision=lax.Precision.HIGHEST)
    panel_of = cols_row // PAN_ROWS
    onehot = (panel_of[:, None] == jnp.arange(N_ROW, dtype=jnp.int32)[None, :]).astype(jnp.float32)
    grouped = jnp.einsum('aq,asxz->qsxz', onehot, pieces, precision=lax.Precision.HIGHEST).astype(jnp.bfloat16)
    return jnp.sum(grouped.astype(jnp.float32), axis=0).astype(jnp.bfloat16)


def reference(left_blocks, left_cols, reach_blocks, reach_cols):
    flat_blocks = left_blocks.reshape((N_ROW * SLAB_PAN, KEPT, BLK, BLK))
    flat_cols = left_cols.reshape((N_ROW * SLAB_PAN, KEPT))

    def single(bundle):
        return slab_row(bundle[0], bundle[1], reach_blocks, reach_cols)

    result = lax.map(single, (flat_blocks, flat_cols))
    return result.reshape((N_ROW, SLAB_PAN, KEPT, BLK, BLK))
```

```python
import functools

import jax
import jax.numpy as jnp
from jax import lax
from jax.experimental import pallas as pl
from jax.experimental.pallas import tpu as pltpu
from jax.sharding import PartitionSpec as P

BLK = 128
NZ, NY, NX, NC = 8, 4, 4, 2
KEPT = 32
HALF = 4
SEL = 8
SET = 128
ZERO = 2 * SET
AXES = ("row", "col")
OFFSETS = (2, 1, -1, 0)


def send(block, target):
    pairs = []
    for z in range(NZ):
        for y in range(NY):
            for x in range(NX):
                for c in range(NC):
                    tz, ty, tx, tc = target(z, y, x, c)
                    tz, ty, tx = tz % NZ, ty % NY, tx % NX
                    src = ((z * NY + y) * NX + x) * NC + c
                    dst = ((tz * NY + ty) * NX + tx) * NC + tc
                    pairs.append((src, dst))
    return lax.ppermute(block, AXES, pairs)


def swap(block):
    return send(block, lambda z, y, x, c: (z, y, x, 1 - c))


def along_z(block, distance):
    return send(block, lambda z, y, x, c: (z + distance * (1 - 2 * c), y, x, c))


def in_plane(block, distance, flip):
    def target(z, y, x, c):
        if c ^ flip:
            return (z, y + distance, x, c)
        return (z, y, x + distance, c)

    return send(block, target)


def ring(block, flip):
    half = block.shape[0] // 2
    up = in_plane(block, 1, flip)
    down = in_plane(block, -1, flip)
    up2 = in_plane(up[:half], 1, flip)
    down2 = in_plane(down[half:], -1, flip)
    return (up, down, up2, down2)


def plane_gather(block, flip):
    first = jnp.concatenate((block,) + ring(block, flip), axis=0)
    return (first,) + ring(first, 1 - flip)


def products_kernel(n_rows, n_add, row_srcs, idx_ref, order_ref, count_ref, *refs):
    n_left = max(src for src, _ in row_srcs) + 1
    panel_refs = refs[:10]
    left_refs = refs[10:10 + n_left]
    add_refs = refs[10 + n_left:10 + n_left + n_add]
    out_ref, panel, lcat, panel_sem, left_sem = refs[10 + n_left + n_add:]
    copies = []
    at = 0
    for n, ref in enumerate(panel_refs):
        size = ref.shape[0]
        copies.append(pltpu.make_async_copy(ref, panel.at[pl.ds(at, size)], panel_sem.at[n]))
        at += size
    for copy in copies:
        copy.start()
    left_copies = []
    for r, (src, base) in enumerate(row_srcs):
        for t in range(SEL):
            which = order_ref[r * SEL + t]
            copy = pltpu.make_async_copy(
                left_refs[src].at[base + which],
                lcat.at[r, :, pl.ds(t * BLK, BLK)],
                left_sem.at[r, t],
            )
            copy.start()
            left_copies.append(copy)
    panel[ZERO] = jnp.zeros((BLK, BLK), panel.dtype)
    for copy in left_copies:
        copy.wait()
    for copy in copies:
        copy.wait()
    for r in range(n_rows):
        pairs_here = (count_ref[r] + 1) // 2
        for pairs in range(SEL // 2 + 1):

            @pl.when(pairs_here == pairs)
            def _(r=r, pairs=pairs):
                def step(sp, carry):
                    s0 = 2 * sp
                    s1 = s0 + 1
                    if pairs:
                        strips = []
                        for t in range(2 * pairs):
                            at0 = idx_ref[(r * SEL + t) * KEPT + s0]
                            at1 = idx_ref[(r * SEL + t) * KEPT + s1]
                            strips.append(jnp.concatenate([panel[at0], panel[at1]], axis=1))
                        rhs = jnp.concatenate(strips, axis=0)
                        total = jnp.dot(
                            lcat[r, :, : 2 * pairs * BLK], rhs, preferred_element_type=jnp.float32
                        )
                    else:
                        total = jnp.zeros((BLK, 2 * BLK), jnp.float32)
                    first = total[:, :BLK]
                    second = total[:, BLK:]
                    for add in add_refs:
                        first = first + add[r, s0].astype(jnp.float32)
                        second = second + add[r, s1].astype(jnp.float32)
                    out_ref[r, s0] = first.astype(out_ref.dtype)
                    out_ref[r, s1] = second.astype(out_ref.dtype)
                    return carry

                lax.fori_loop(0, KEPT // 2, step, 0)


def products(tables, rows, panel_parts, lefts, row_srcs, adds, dtype=jnp.bfloat16):
    idx, order, count = tables
    n = len(rows)
    pick = jnp.array(rows, dtype=jnp.int32)
    idx = idx[pick].reshape(-1)
    order = order[pick].reshape(-1)
    count = count[pick]
    smem = pl.BlockSpec(memory_space=pltpu.SMEM)
    hbm = pl.BlockSpec(memory_space=pl.ANY)
    vmem = pl.BlockSpec(memory_space=pltpu.VMEM)
    return pl.pallas_call(
        functools.partial(products_kernel, n, len(adds), row_srcs),
        out_shape=jax.ShapeDtypeStruct((n, KEPT, BLK, BLK), dtype),
        in_specs=[smem] * 3 + [hbm] * (len(panel_parts) + len(lefts)) + [vmem] * len(adds),
        out_specs=vmem,
        scratch_shapes=[
            pltpu.VMEM((ZERO + 1, BLK, BLK), jnp.bfloat16),
            pltpu.VMEM((n, BLK, SEL * BLK), jnp.bfloat16),
            pltpu.SemaphoreType.DMA((len(panel_parts),)),
            pltpu.SemaphoreType.DMA((n, SEL)),
        ],
        compiler_params=pltpu.CompilerParams(vmem_limit_bytes=40 * 1024 * 1024),
        cost_estimate=pl.CostEstimate(
            flops=n * KEPT * SEL * 2 * BLK**3, bytes_accessed=10 * 1024 * 1024, transcendentals=0
        ),
    )(idx, order, count, *panel_parts, *lefts, *adds)


def reached(z, c):
    j = jnp.arange(SEL, dtype=jnp.int32)
    panel = (z + NZ // 2 * (j // HALF)) % NZ
    return panel * (2 * HALF) + c * HALF + j % HALF


def local(left_blocks, left_cols, reach_blocks, reach_cols):
    z = lax.axis_index("row")
    col = lax.axis_index("col")
    c = col % NC
    x = col // NC % NX
    y = col // (NC * NX)
    sign = 1 - 2 * c

    blocks = reach_blocks[:, 0]
    own_half = lax.dynamic_slice_in_dim(blocks, HALF * c, HALF, 0)
    other_half = lax.dynamic_slice_in_dim(blocks, HALF * (1 - c), HALF, 0)
    near_set = jnp.concatenate([own_half, swap(other_half)], axis=0)
    far_set = send(near_set, lambda z, y, x, c: (z + NZ // 2, y, x, c))
    panel_parts = plane_gather(near_set, 0) + plane_gather(far_set, 1)

    own_left = left_blocks[0, 0]
    own_cols = lax.dynamic_index_in_dim(left_cols[:, 0], z, 0, keepdims=False)

    def chosen(offset):
        target = z + offset * sign + NZ
        names = jnp.concatenate([reached(target, c), reached(target, 1 - c)])
        at = jnp.argmax(names[:, None] == own_cols[None, :], axis=1).astype(jnp.int32)
        return own_left[at]

    arrived = []
    for offset in OFFSETS:
        picked = chosen(offset)
        arrived.append(along_z(picked, offset) if offset else picked)
    swapped = swap(jnp.concatenate([a[SEL:] for a in arrived], axis=0))

    cols_here = left_cols[:, 0]
    cols_there = swap(cols_here)
    steps = jnp.array(OFFSETS, dtype=jnp.int32)
    cols = jnp.concatenate(
        [cols_there[(z + steps * sign + NZ) % NZ], cols_here[(z - steps * sign + NZ) % NZ]], axis=0
    )
    far_cols = send(reach_cols, lambda z, y, x, c: (z + NZ // 2, y, x, c))
    kept = jnp.concatenate(
        [
            lax.dynamic_slice_in_dim(reach_cols, HALF * c, HALF, 0),
            lax.dynamic_slice_in_dim(far_cols, HALF * c, HALF, 0),
        ],
        axis=0,
    )
    slot = jnp.arange(KEPT, dtype=jnp.int32)

    def place(offset):
        offset = offset % 4
        return jnp.where(offset == 0, 0, jnp.where(offset == 3, 1, jnp.where(offset == 1, 2, 3)))

    dx = place(slot // NC % NX - x + NX)
    dy = place(slot // (NC * NX) - y + NY)
    other = jnp.where(slot % NC == c, 0, 1)
    along = jnp.where(c == 0, dx, dy)
    across = jnp.where(c == 0, dy, dx)
    j = jnp.arange(SEL, dtype=jnp.int32)
    near_place = across * 32 + along * 8 + other * HALF
    far_place = along * 32 + across * 8 + other * HALF + SET
    place_of = jnp.where(j[:, None] < HALF, near_place[None, :], far_place[None, :]) + j[:, None] % HALF
    present = jnp.any(reached(z, c)[None, :, None] == cols[:, None, :], axis=2)
    rank = jnp.cumsum(present.astype(jnp.int32), axis=1) - 1
    hit = present[:, None, :] & (rank[:, None, :] == j[None, :, None])
    order = jnp.sum(jnp.where(hit, j[None, None, :], 0), axis=2)
    same = kept[None, :, None, :] == cols[:, None, :, None]
    at = jnp.sum(jnp.where(same, place_of[None, :, None, :] - ZERO, 0), axis=3)
    idx = ZERO + jnp.sum(jnp.where(hit[:, :, :, None], at[:, None, :, :], 0), axis=2)
    count = jnp.sum(present.astype(jnp.int32), axis=1)
    tables = (idx, order, count)

    call = functools.partial(products, tables)
    far_l, near_l, leaf_l, own_l = arrived
    far_there = call((0,), panel_parts, (swapped,), ((0, 0),), ())
    far_here = call((4,), panel_parts, (far_l,), ((0, 0),), (swap(far_there),))
    far_got = along_z(far_here, -1)
    rest_there = call((1, 2, 3), panel_parts, (swapped,), ((0, 8), (0, 16), (0, 24)), ())
    rest_got = swap(rest_there)
    rest_here = call(
        (6, 7), panel_parts, (leaf_l, own_l), ((0, 0), (1, 0)), (rest_got[1:],)
    )
    leaf_got = along_z(rest_here[:1], 1)
    near_here = call((5,), panel_parts, (near_l,), ((0, 0),), (rest_got[:1], far_got))
    near_got = along_z(near_here, -1)
    total = (
        rest_here[1].astype(jnp.float32)
        + leaf_got[0].astype(jnp.float32)
        + near_got[0].astype(jnp.float32)
    )
    return total.astype(jnp.bfloat16)[None, None]


def solution(mesh):
    in_specs = (
        P("row", "col", None, None, None),
        P(None, "col", None),
        P("row", "col", None, None),
        P("row", None),
    )
    out_specs = P("row", "col", None, None, None)
    return jax.shard_map(local, mesh=mesh, in_specs=in_specs, out_specs=out_specs, check_vma=False)
```

```python
import functools

import jax
import jax.numpy as jnp
from jax import lax
from jax.experimental import pallas as pl
from jax.experimental.pallas import tpu as pltpu
from jax.sharding import PartitionSpec as P

BLK = 128
NZ, NY, NX, NC = 8, 4, 4, 2
KEPT = 32
ROWS = 8
SEL = 16
SET = 256
AXES = ("row", "col")
OFFSETS = (2, 1, -1, 0)


def send(block, target):
    pairs = []
    for z in range(NZ):
        for y in range(NY):
            for x in range(NX):
                for c in range(NC):
                    tz, ty, tx, tc = target(z, y, x, c)
                    tz, ty, tx = tz % NZ, ty % NY, tx % NX
                    src = ((z * NY + y) * NX + x) * NC + c
                    dst = ((tz * NY + ty) * NX + tx) * NC + tc
                    pairs.append((src, dst))
    return lax.ppermute(block, AXES, pairs)


def swap(block):
    return send(block, lambda z, y, x, c: (z, y, x, 1 - c))


def along_z(block, distance):
    return send(block, lambda z, y, x, c: (z + distance * (1 - 2 * c), y, x, c))


def in_plane(block, distance, flip):
    def target(z, y, x, c):
        if c ^ flip:
            return (z, y + distance, x, c)
        return (z, y, x + distance, c)

    return send(block, target)


def pack_kernel(size, starts_ref, *refs):
    parts, out_ref = refs[:-1], refs[-1]
    for n, ref in enumerate(parts):
        for i in range(size):
            out_ref[n * size + i] = ref[starts_ref[n] + i]


def pack(parts, size, starts=None):
    if starts is None:
        starts = jnp.zeros((len(parts),), jnp.int32)
    total = size * len(parts)
    vmem = pl.BlockSpec(memory_space=pltpu.VMEM)
    return pl.pallas_call(
        functools.partial(pack_kernel, size),
        out_shape=jax.ShapeDtypeStruct((total, BLK, BLK), jnp.bfloat16),
        in_specs=[pl.BlockSpec(memory_space=pltpu.SMEM)] + [vmem] * len(parts),
        out_specs=vmem,
        compiler_params=pltpu.CompilerParams(vmem_limit_bytes=8 * 1024 * 1024),
        cost_estimate=pl.CostEstimate(
            flops=0, bytes_accessed=4 * total * BLK * BLK, transcendentals=0
        ),
        name="pack",
    )(starts, *parts)


def pick_kernel(at_ref, blocks_ref, *outs):
    for n, out in enumerate(outs):
        for i in range(SEL):
            out[i] = blocks_ref[at_ref[n * SEL + i]]


def pick(blocks, at):
    n = len(OFFSETS)
    vmem = pl.BlockSpec(memory_space=pltpu.VMEM)
    return pl.pallas_call(
        pick_kernel,
        out_shape=[jax.ShapeDtypeStruct((SEL, BLK, BLK), jnp.bfloat16)] * n,
        in_specs=[pl.BlockSpec(memory_space=pltpu.SMEM), vmem],
        out_specs=[vmem] * n,
        compiler_params=pltpu.CompilerParams(vmem_limit_bytes=8 * 1024 * 1024),
        cost_estimate=pl.CostEstimate(
            flops=0, bytes_accessed=4 * n * SEL * BLK * BLK, transcendentals=0
        ),
        name="pick",
    )(at, blocks)


def products_kernel(n_panel, n_left, base, n_add, idx_ref, order_ref, count_ref, *refs):
    panel_refs, refs = refs[:n_panel], refs[n_panel:]
    left_refs, refs = refs[:n_left], refs[n_left:]
    add_ref = refs[0] if n_add else None
    out_ref, panel, lefts, panel_sem, left_sem = refs[n_add:]
    copies = []
    at = 0
    for n, ref in enumerate(panel_refs):
        size = ref.shape[0]
        copies.append(pltpu.make_async_copy(ref, panel.at[pl.ds(at, size)], panel_sem.at[n]))
        at += size
    for r, ref in enumerate(left_refs):
        copies.append(
            pltpu.make_async_copy(ref.at[pl.ds(base, ROWS)], lefts.at[r], left_sem.at[r])
        )
    for copy in copies:
        copy.start()
    panel[SET] = jnp.zeros((BLK, BLK), panel.dtype)
    for copy in copies:
        copy.wait()

    def row(r, carry):
        pairs_here = (count_ref[r] + 1) // 2
        for pairs in range(ROWS // 2 + 1):

            @pl.when(pairs_here == pairs)
            def _(pairs=pairs):
                def step(sp, inner):
                    s0 = 2 * sp
                    if pairs:
                        strips = []
                        for t in range(2 * pairs):
                            spot = (r * ROWS + t) * KEPT + s0
                            strips.append(
                                jnp.concatenate(
                                    [panel[idx_ref[spot]], panel[idx_ref[spot + 1]]], axis=1
                                )
                            )
                        lhs = jnp.concatenate(
                            [lefts[r, order_ref[r * ROWS + t]] for t in range(2 * pairs)], axis=1
                        )
                        total = jnp.dot(
                            lhs,
                            jnp.concatenate(strips, axis=0),
                            preferred_element_type=jnp.float32,
                        )
                    else:
                        total = jnp.zeros((BLK, 2 * BLK), jnp.float32)
                    both = [total[:, :BLK], total[:, BLK:]]
                    for k in range(2):
                        if n_add:
                            both[k] = both[k] + add_ref[r, s0 + k].astype(jnp.float32)
                        out_ref[r, s0 + k] = both[k].astype(out_ref.dtype)
                    return inner

                lax.fori_loop(0, KEPT // 2, step, 0, unroll=8)

        return carry

    lax.fori_loop(0, n_left, row, 0)


def products(table, panel_parts, lefts, base, add=None):
    n = len(lefts)
    adds = () if add is None else (add,)
    smem = pl.BlockSpec(memory_space=pltpu.SMEM)
    hbm = pl.BlockSpec(memory_space=pl.ANY)
    vmem = pl.BlockSpec(memory_space=pltpu.VMEM)
    return pl.pallas_call(
        functools.partial(products_kernel, len(panel_parts), n, base, len(adds)),
        out_shape=jax.ShapeDtypeStruct((n, KEPT, BLK, BLK), jnp.bfloat16),
        in_specs=[smem] * 3
        + [pl.BlockSpec(memory_space=pltpu.HBM)]
        + [hbm] * (len(panel_parts) - 1 + n)
        + [vmem] * len(adds),
        out_specs=vmem,
        scratch_shapes=[
            pltpu.VMEM((SET + 1, BLK, BLK), jnp.bfloat16),
            pltpu.VMEM((n, ROWS, BLK, BLK), jnp.bfloat16),
            pltpu.SemaphoreType.DMA((len(panel_parts),)),
            pltpu.SemaphoreType.DMA((n,)),
        ],
        compiler_params=pltpu.CompilerParams(vmem_limit_bytes=24 * 1024 * 1024),
        cost_estimate=pl.CostEstimate(
            flops=n * KEPT * ROWS * 2 * BLK**3,
            bytes_accessed=8 * 1024 * 1024,
            transcendentals=0,
        ),
        name="products",
    )(*table, *(pltpu.with_memory_space_constraint(a, pltpu.HBM) for a in panel_parts[:1]), *panel_parts[1:], *lefts, *adds)


def plus_kernel(rows, *refs):
    out_ref = refs[-1]

    def step(i, carry):
        total = refs[0][rows[0], i].astype(jnp.float32)
        for row, ref in zip(rows[1:], refs[1:-1]):
            total = total + ref[row, i].astype(jnp.float32)
        out_ref[0, i] = total.astype(out_ref.dtype)
        return carry

    lax.fori_loop(0, KEPT, step, 0, unroll=4)


def plus(*terms):
    vmem = pl.BlockSpec(memory_space=pltpu.VMEM)
    return pl.pallas_call(
        functools.partial(plus_kernel, tuple(row for _, row in terms)),
        out_shape=jax.ShapeDtypeStruct((1, KEPT, BLK, BLK), jnp.bfloat16),
        in_specs=[vmem] * len(terms),
        out_specs=vmem,
        compiler_params=pltpu.CompilerParams(vmem_limit_bytes=16 * 1024 * 1024),
        cost_estimate=pl.CostEstimate(
            flops=0, bytes_accessed=(len(terms) + 1) * KEPT * BLK * BLK * 2, transcendentals=0
        ),
        name="plus",
    )(*(array for array, _ in terms))


def stage(*arrays):
    return lax.optimization_barrier(arrays)


def reached(z):
    j = jnp.arange(SEL, dtype=jnp.int32)
    return (z + NZ // 2 * (j // ROWS)) % NZ * ROWS + j % ROWS


def local(left_blocks, left_cols, reach_blocks, reach_cols):
    z = lax.axis_index("row")
    col = lax.axis_index("col")
    c = col % NC
    x = col // NC % NX
    y = col // (NC * NX)
    sign = 1 - 2 * c
    blocks = reach_blocks[:, 0]

    near_panel = lax.all_gather(blocks, "col", axis=0, tiled=True)

    own_left = left_blocks[0, 0]
    cols_here = left_cols[:, 0]
    own_cols = lax.dynamic_index_in_dim(cols_here, z, 0, keepdims=False)
    names = jnp.concatenate([reached(z + offset * sign + NZ) for offset in OFFSETS])
    picked_at = jnp.argmax(names[:, None] == own_cols[None, :], axis=1)

    far_l, near_l, leaf_l, own_l = pick(own_left, picked_at.astype(jnp.int32))
    far_set, far_l, near_l, leaf_l, own_l, reach_cols = stage(
        send(blocks, lambda z, y, x, c: (z + NZ // 2, y, x, c)),
        far_l,
        near_l,
        leaf_l,
        own_l,
        reach_cols,
    )
    ring = [in_plane(far_set, distance, 0) for distance in (1, -1, 2)]
    far_cols = send(reach_cols, lambda z, y, x, c: (z + NZ // 2, y, x, c))
    far_set, ring = stage(far_set, ring)
    far_l = along_z(far_l, 2)

    steps = jnp.array(OFFSETS, dtype=jnp.int32)
    cols = cols_here[(z - steps * sign + NZ) % NZ]
    slot = jnp.arange(KEPT, dtype=jnp.int32)

    def place(offset):
        offset = offset % 4
        return jnp.where(offset == 0, 0, jnp.where(offset == 3, 1, jnp.where(offset == 1, 2, 3)))

    dx = place(slot // NC % NX - x + NX)
    dy = place(slot // (NC * NX) - y + NY)
    first, then = jnp.where(slot % NC == 0, dx, dy), jnp.where(slot % NC == 0, dy, dx)
    far_place = jnp.where(slot % NC == c, 0, SET // 2) + then * 32 + first * 8
    j = jnp.arange(ROWS, dtype=jnp.int32)
    here = reached(z)

    def table(kept, places, names):
        place_of = places[None, :] + j[:, None]
        present = jnp.any(names[None, :, None] == cols[:, None, :], axis=2)
        rank = jnp.sum(present[:, None, :] & (j[None, None, :] < j[None, :, None]), axis=2)
        hit = present[:, None, :] & (rank[:, None, :] == j[None, :, None])
        order = jnp.sum(jnp.where(hit, j[None, None, :], 0), axis=2)
        same = kept[None, :, None, :] == cols[:, None, :, None]
        at = jnp.sum(jnp.where(same, place_of[None, :, None, :] - SET, 0), axis=3)
        idx = SET + jnp.sum(jnp.where(hit[:, :, :, None], at[:, None, :, :], 0), axis=2)
        return idx, order, jnp.sum(present.astype(jnp.int32), axis=1)

    def rows(tables, first, last):
        return tuple(t[first:last].reshape(-1) for t in tables)

    near_table = table(reach_cols, slot * ROWS, here[:ROWS])
    far_table = table(far_cols, far_place, here[ROWS:])
    tables = [rows(t, *span) for t in (near_table, far_table) for span in ((0, 1), (1, 4))]

    first = pack((far_set, *ring), ROWS)
    first, up, down, far_l, near_l, leaf_l, first_got, tables = stage(
        first,
        in_plane(first, 1, 1),
        in_plane(first, -1, 1),
        far_l,
        along_z(near_l, 1),
        along_z(leaf_l, -1),
        swap(first),
        tables,
    )
    half = 2 * ROWS
    last = (
        in_plane(pack((up,), half), 1, 1),
        in_plane(pack((down,), half, jnp.full((1,), half, jnp.int32)), -1, 1),
    )
    lefts = (near_l, leaf_l, own_l)
    near_far = products(tables[0], (near_panel,), (far_l,), 0)
    up_got, down_got, last, near_far = stage(swap(up), swap(down), last, near_far)
    own_parts = (first, up, down, *last)
    got_parts = (first_got, up_got, down_got, swap(last[0]), swap(last[1]))
    far_panel = (*own_parts, *got_parts)

    far_term = products(tables[2], far_panel, (far_l,), ROWS, near_far)
    far_got = along_z(far_term, -1)
    near_panel, far_term = stage(near_panel, far_term)
    near_rest = products(tables[1], (near_panel,), lefts, 0)
    terms = products(tables[3], far_panel, lefts, ROWS, near_rest)
    leaf_got = along_z(terms[1:2], 1)
    near_got = along_z(plus((terms, 0), (far_got, 0)), -1)
    return plus((terms, 2), (leaf_got, 0), (near_got, 0))[None]


def solution(mesh):
    in_specs = (
        P("row", "col", None, None, None),
        P(None, "col", None),
        P("row", "col", None, None),
        P("row", None),
    )
    out_specs = P("row", "col", None, None, None)
    return jax.shard_map(local, mesh=mesh, in_specs=in_specs, out_specs=out_specs, check_vma=False)
```

```python
import functools

import jax
import jax.numpy as jnp
from jax import lax
from jax.experimental import pallas as pl
from jax.experimental.pallas import tpu as pltpu
from jax.sharding import PartitionSpec as P

BLK = 128
NZ, NY, NX, NC = 8, 4, 4, 2
KEPT = 32
ROWS = 8
SEL = 16
SET = 512
AXES = ("row", "col")
OFFSETS = (2, 1, -1, 0)


def send(block, target):
    pairs = []
    for z in range(NZ):
        for y in range(NY):
            for x in range(NX):
                for c in range(NC):
                    tz, ty, tx, tc = target(z, y, x, c)
                    tz, ty, tx = tz % NZ, ty % NY, tx % NX
                    src = ((z * NY + y) * NX + x) * NC + c
                    dst = ((tz * NY + ty) * NX + tx) * NC + tc
                    pairs.append((src, dst))
    return lax.ppermute(block, AXES, pairs)


def swap(block):
    return send(block, lambda z, y, x, c: (z, y, x, 1 - c))


def along_z(block, distance):
    return send(block, lambda z, y, x, c: (z + distance * (1 - 2 * c), y, x, c))


def in_plane(block, distance, flip):
    def target(z, y, x, c):
        if c ^ flip:
            return (z, y + distance, x, c)
        return (z, y, x + distance, c)

    return send(block, target)


def join_kernel(*refs):
    parts, out_ref, sems = refs[:-2], refs[-2], refs[-1]
    copies = []
    at = 0
    for n, ref in enumerate(parts):
        size = ref.shape[0]
        copies.append(pltpu.make_async_copy(ref, out_ref.at[pl.ds(at, size)], sems.at[n]))
        at += size
    for copy in copies:
        copy.start()
    for copy in copies:
        copy.wait()


def join(parts, others):
    total = sum(part.shape[0] for part in parts + others)
    return pl.pallas_call(
        join_kernel,
        out_shape=jax.ShapeDtypeStruct((total, BLK, BLK), jnp.bfloat16),
        in_specs=[pl.BlockSpec(memory_space=pltpu.HBM)] * len(parts)
        + [pl.BlockSpec(memory_space=pl.ANY)] * len(others),
        out_specs=pl.BlockSpec(memory_space=pltpu.VMEM),
        scratch_shapes=[pltpu.SemaphoreType.DMA((len(parts + others),))],
        compiler_params=pltpu.CompilerParams(vmem_limit_bytes=4 * 1024 * 1024),
        cost_estimate=pl.CostEstimate(
            flops=0, bytes_accessed=4 * total * BLK * BLK, transcendentals=0
        ),
        name="join",
    )(*(pltpu.with_memory_space_constraint(part, pltpu.HBM) for part in parts), *others)


def halves_kernel(up_ref, down_ref, first_ref, second_ref, sems):
    half = first_ref.shape[0]
    copies = [
        pltpu.make_async_copy(up_ref.at[pl.ds(0, half)], first_ref, sems.at[0]),
        pltpu.make_async_copy(down_ref.at[pl.ds(half, half)], second_ref, sems.at[1]),
    ]
    for copy in copies:
        copy.start()
    for copy in copies:
        copy.wait()


def halves(up, down):
    half = up.shape[0] // 2
    hbm = pl.BlockSpec(memory_space=pl.ANY)
    return pl.pallas_call(
        halves_kernel,
        out_shape=[jax.ShapeDtypeStruct((half, BLK, BLK), jnp.bfloat16)] * 2,
        in_specs=[hbm] * 2,
        out_specs=[hbm] * 2,
        scratch_shapes=[pltpu.SemaphoreType.DMA((2,))],
        compiler_params=pltpu.CompilerParams(vmem_limit_bytes=1024 * 1024),
        cost_estimate=pl.CostEstimate(
            flops=0, bytes_accessed=8 * half * BLK * BLK, transcendentals=0
        ),
        name="halves",
    )(up, down)


def pick_kernel(at_ref, blocks_ref, *outs):
    for n, out in enumerate(outs):
        for i in range(SEL):
            out[i] = blocks_ref[at_ref[n * SEL + i]]


def pick(blocks, at):
    n = len(OFFSETS)
    vmem = pl.BlockSpec(memory_space=pltpu.VMEM)
    return pl.pallas_call(
        pick_kernel,
        out_shape=[jax.ShapeDtypeStruct((SEL, BLK, BLK), jnp.bfloat16)] * n,
        in_specs=[pl.BlockSpec(memory_space=pltpu.SMEM), vmem],
        out_specs=[vmem] * n,
        compiler_params=pltpu.CompilerParams(vmem_limit_bytes=8 * 1024 * 1024),
        cost_estimate=pl.CostEstimate(
            flops=0, bytes_accessed=4 * n * SEL * BLK * BLK, transcendentals=0
        ),
        name="pick",
    )(at, blocks)


def products_kernel(n_panel, n_left, n_add, idx_ref, order_ref, count_ref, *refs):
    panel_refs, refs = refs[:n_panel], refs[n_panel:]
    left_refs, refs = refs[:n_left], refs[n_left:]
    add_refs, out_refs = refs[:n_add], refs[n_add:-4]
    panel, lefts, panel_sem, left_sem = refs[-4:]
    copies = []
    at = 0
    for n, ref in enumerate(panel_refs):
        size = ref.shape[0]
        copies.append(pltpu.make_async_copy(ref, panel.at[pl.ds(at, size)], panel_sem.at[n]))
        at += size
    for r, ref in enumerate(left_refs):
        copies.append(pltpu.make_async_copy(ref, lefts.at[r], left_sem.at[r]))
    for copy in copies:
        copy.start()
    panel[at] = jnp.zeros((BLK, BLK), panel.dtype)
    for copy in copies:
        copy.wait()
    for r in range(n_left):
        pairs_here = (count_ref[r] + 1) // 2
        for pairs in range(SEL // 2 + 1):

            @pl.when(pairs_here == pairs)
            def _(r=r, pairs=pairs):
                def step(sp, inner):
                    s0 = 2 * sp
                    if pairs:
                        strips = []
                        for t in range(2 * pairs):
                            spot = (r * SEL + t) * KEPT + s0
                            strips.append(
                                jnp.concatenate(
                                    [panel[idx_ref[spot]], panel[idx_ref[spot + 1]]], axis=1
                                )
                            )
                        lhs = jnp.concatenate(
                            [lefts[r, order_ref[r * SEL + t]] for t in range(2 * pairs)], axis=1
                        )
                        total = jnp.dot(
                            lhs,
                            jnp.concatenate(strips, axis=0),
                            preferred_element_type=jnp.float32,
                        )
                    else:
                        total = jnp.zeros((BLK, 2 * BLK), jnp.float32)
                    both = [total[:, :BLK], total[:, BLK:]]
                    for k in range(2):
                        if n_add:
                            both[k] = both[k] + add_refs[r][0, s0 + k].astype(jnp.float32)
                        out_refs[r][0, s0 + k] = both[k].astype(jnp.bfloat16)
                    return inner

                lax.fori_loop(0, KEPT // 2, step, 0, unroll=4)


def products(table, panel_parts, lefts, adds=()):
    n = len(lefts)
    total = sum(part.shape[0] for part in panel_parts)
    smem = pl.BlockSpec(memory_space=pltpu.SMEM)
    hbm = pl.BlockSpec(memory_space=pl.ANY)
    vmem = pl.BlockSpec(memory_space=pltpu.VMEM)
    return pl.pallas_call(
        functools.partial(products_kernel, len(panel_parts), n, len(adds)),
        out_shape=[jax.ShapeDtypeStruct((1, KEPT, BLK, BLK), jnp.bfloat16)] * n,
        in_specs=[smem] * 3 + [hbm] * (len(panel_parts) + n) + [vmem] * len(adds),
        out_specs=[vmem] * n,
        scratch_shapes=[
            pltpu.VMEM((total + 1, BLK, BLK), jnp.bfloat16),
            pltpu.VMEM((n, SEL, BLK, BLK), jnp.bfloat16),
            pltpu.SemaphoreType.DMA((len(panel_parts),)),
            pltpu.SemaphoreType.DMA((n,)),
        ],
        compiler_params=pltpu.CompilerParams(vmem_limit_bytes=24 * 1024 * 1024),
        cost_estimate=pl.CostEstimate(
            flops=n * KEPT * SEL * 2 * BLK**3,
            bytes_accessed=total * BLK * BLK * 2,
            transcendentals=0,
        ),
        name="products",
    )(*table, *panel_parts, *lefts, *adds)


def plus_kernel(rows, *refs):
    out_ref = refs[-1]

    def step(i, carry):
        total = refs[0][rows[0], i].astype(jnp.float32)
        for row, ref in zip(rows[1:], refs[1:-1]):
            total = total + ref[row, i].astype(jnp.float32)
        out_ref[0, i] = total.astype(out_ref.dtype)
        return carry

    lax.fori_loop(0, KEPT, step, 0, unroll=4)


def plus(*terms):
    vmem = pl.BlockSpec(memory_space=pltpu.VMEM)
    return pl.pallas_call(
        functools.partial(plus_kernel, tuple(row for _, row in terms)),
        out_shape=jax.ShapeDtypeStruct((1, KEPT, BLK, BLK), jnp.bfloat16),
        in_specs=[vmem] * len(terms),
        out_specs=vmem,
        compiler_params=pltpu.CompilerParams(vmem_limit_bytes=16 * 1024 * 1024),
        cost_estimate=pl.CostEstimate(
            flops=0, bytes_accessed=(len(terms) + 1) * KEPT * BLK * BLK * 2, transcendentals=0
        ),
        name="plus",
    )(*(array for array, _ in terms))


def stage(*arrays):
    return lax.optimization_barrier(arrays)


def reached(z):
    j = jnp.arange(SEL, dtype=jnp.int32)
    return (z + NZ // 2 * (j // ROWS)) % NZ * ROWS + j % ROWS


def local(left_blocks, left_cols, reach_blocks, reach_cols):
    z = lax.axis_index("row")
    col = lax.axis_index("col")
    c = col % NC
    x = col // NC % NX
    y = col // (NC * NX)
    sign = 1 - 2 * c
    blocks = reach_blocks[:, 0]

    own_left = left_blocks[0, 0]
    cols_here = left_cols[:, 0]
    own_cols = lax.dynamic_index_in_dim(cols_here, z, 0, keepdims=False)
    names = jnp.concatenate([reached(z + offset * sign + NZ) for offset in OFFSETS])
    picked_at = jnp.argmax(names[:, None] == own_cols[None, :], axis=1)

    def round_one(block):
        return [in_plane(block, distance, 0) for distance in (1, -1, 2)]

    near_ring, picked, reach_cols, far_set = stage(
        round_one(blocks),
        pick(own_left, picked_at.astype(jnp.int32)),
        reach_cols,
        send(blocks, lambda z, y, x, c: (z + NZ // 2, y, x, c)),
    )
    far_l, near_l, leaf_l, own_l = picked
    far_l = along_z(far_l, 2)
    far_cols, far_ring, leaf_l = stage(
        send(reach_cols, lambda z, y, x, c: (z + NZ // 2, y, x, c)), round_one(far_set), leaf_l
    )
    first = join((blocks, *near_ring), (far_set, *far_ring))

    steps = jnp.array(OFFSETS, dtype=jnp.int32)
    cols = cols_here[(z - steps * sign + NZ) % NZ]
    slot = jnp.arange(KEPT, dtype=jnp.int32)

    def place(offset):
        offset = offset % 4
        return jnp.where(offset == 0, 0, jnp.where(offset == 3, 1, jnp.where(offset == 1, 2, 3)))

    dx = place(slot // NC % NX - x + NX)
    dy = place(slot // (NC * NX) - y + NY)
    then, ahead = jnp.where(slot % NC == 0, dy, dx), jnp.where(slot % NC == 0, dx, dy)
    turn = jnp.where(slot % NC == c, jnp.where(then == 3, 4, then), jnp.where(then == 0, 3, then + 4))
    near_place = turn * 64 + ahead * 8
    j = jnp.arange(SEL, dtype=jnp.int32)

    kept = jnp.concatenate([reach_cols, far_cols], axis=0)
    place_of = near_place[None, :] + (j // ROWS * 32 + j % ROWS)[:, None]
    present = jnp.any(reached(z)[None, :, None] == cols[:, None, :], axis=2)
    rank = jnp.sum(present[:, None, :] & (j[None, None, :] < j[None, :, None]), axis=2)
    hit = present[:, None, :] & (rank[:, None, :] == j[None, :, None])
    order = jnp.sum(jnp.where(hit, j[None, None, :], 0), axis=2)
    same = kept[None, :, None, :] == cols[:, None, :, None]
    at = jnp.sum(jnp.where(same, place_of[None, :, None, :] - SET, 0), axis=3)
    idx = SET + jnp.sum(jnp.where(hit[:, :, :, None], at[:, None, :, :], 0), axis=2)
    count = jnp.sum(present.astype(jnp.int32), axis=1)
    half = SET // 2
    idx_early = jnp.where(idx < half, idx, half)
    idx_late = jnp.where((idx >= half) & (idx < SET), idx - half, half)

    def entry(blocks_at, first, last):
        return tuple(t[first:last].reshape(-1) for t in (blocks_at, order, count))

    tables = entry(idx_early, 0, 1), entry(idx_late, 0, 1), entry(idx, 1, 3), entry(idx, 3, 4)

    tables, far_l, leaf_l, first_got, first, up, down, near_l = stage(
        tables,
        far_l,
        along_z(leaf_l, -1),
        swap(first),
        first,
        in_plane(first, 1, 1),
        in_plane(first, -1, 1),
        near_l,
    )
    near_half, far_half = halves(up, down)
    up, down, near_l, near_half, far_half = stage(up, down, near_l, near_half, far_half)
    early = (first, up, down, first_got)
    up_got, down_got, near_l, near_on, far_on, early_term = stage(
        swap(up),
        swap(down),
        along_z(near_l, 1),
        in_plane(near_half, 1, 1),
        in_plane(far_half, -1, 1),
        products(tables[0], early, (far_l,)),
    )
    late = (near_on, far_on, up_got, down_got, swap(near_on), swap(far_on))

    (far_term,) = products(tables[1], late, (far_l,), early_term)
    far_got = along_z(far_term, -1)
    near_l, leaf_l, far_term = stage(near_l, leaf_l, far_term)
    near_term, leaf_term = products(tables[2], early + late, (near_l, leaf_l))
    leaf_got = along_z(leaf_term, 1)
    near_got = along_z(plus((near_term, 0), (far_got, 0)), -1)
    own_l, leaf_term = stage(own_l, leaf_term)
    (own_term,) = products(tables[3], early + late, (own_l,))
    return plus((own_term, 0), (leaf_got, 0), (near_got, 0))[None]


def solution(mesh):
    in_specs = (
        P("row", "col", None, None, None),
        P(None, "col", None),
        P("row", "col", None, None),
        P("row", None),
    )
    out_specs = P("row", "col", None, None, None)
    return jax.shard_map(local, mesh=mesh, in_specs=in_specs, out_specs=out_specs, check_vma=False)
```

```python
import functools

import jax
import jax.numpy as jnp
from jax import lax
from jax.experimental import pallas as pl
from jax.experimental.pallas import tpu as pltpu
from jax.sharding import PartitionSpec as P

BLK = 128
NZ, NY, NX, NC = 8, 4, 4, 2
KEPT = 32
ROWS = 8
SEL = 16
SET = 512
EARLY = 384
AXES = ("row", "col")
OFFSETS = (2, 1, -1, 0)


def send(block, target):
    pairs = []
    for z in range(NZ):
        for y in range(NY):
            for x in range(NX):
                for c in range(NC):
                    tz, ty, tx, tc = target(z, y, x, c)
                    tz, ty, tx = tz % NZ, ty % NY, tx % NX
                    src = ((z * NY + y) * NX + x) * NC + c
                    dst = ((tz * NY + ty) * NX + tx) * NC + tc
                    pairs.append((src, dst))
    return lax.ppermute(block, AXES, pairs)


def swap(block):
    return send(block, lambda z, y, x, c: (z, y, x, 1 - c))


def along_z(block, distance):
    return send(block, lambda z, y, x, c: (z + distance * (1 - 2 * c), y, x, c))


def in_plane(block, distance, flip):
    def target(z, y, x, c):
        if c ^ flip:
            return (z, y + distance, x, c)
        return (z, y, x + distance, c)

    return send(block, target)


def join_kernel(*refs):
    parts, out_ref, sems = refs[:-2], refs[-2], refs[-1]
    copies = []
    at = 0
    for n, ref in enumerate(parts):
        size = ref.shape[0]
        copies.append(pltpu.make_async_copy(ref, out_ref.at[pl.ds(at, size)], sems.at[n]))
        at += size
    for copy in copies:
        copy.start()
    for copy in copies:
        copy.wait()


def join(parts, others):
    total = sum(part.shape[0] for part in parts + others)
    return pl.pallas_call(
        join_kernel,
        out_shape=jax.ShapeDtypeStruct((total, BLK, BLK), jnp.bfloat16),
        in_specs=[pl.BlockSpec(memory_space=pltpu.HBM)] * len(parts)
        + [pl.BlockSpec(memory_space=pl.ANY)] * len(others),
        out_specs=pl.BlockSpec(memory_space=pltpu.VMEM),
        scratch_shapes=[pltpu.SemaphoreType.DMA((len(parts + others),))],
        compiler_params=pltpu.CompilerParams(vmem_limit_bytes=4 * 1024 * 1024),
        cost_estimate=pl.CostEstimate(
            flops=0, bytes_accessed=4 * total * BLK * BLK, transcendentals=0
        ),
        name="join",
    )(*(pltpu.with_memory_space_constraint(part, pltpu.HBM) for part in parts), *others)


def halves_kernel(up_ref, down_ref, first_ref, second_ref, sems):
    half = first_ref.shape[0]
    copies = [
        pltpu.make_async_copy(up_ref.at[pl.ds(0, half)], first_ref, sems.at[0]),
        pltpu.make_async_copy(down_ref.at[pl.ds(half, half)], second_ref, sems.at[1]),
    ]
    for copy in copies:
        copy.start()
    for copy in copies:
        copy.wait()


def halves(up, down):
    half = up.shape[0] // 2
    hbm = pl.BlockSpec(memory_space=pl.ANY)
    return pl.pallas_call(
        halves_kernel,
        out_shape=[jax.ShapeDtypeStruct((half, BLK, BLK), jnp.bfloat16)] * 2,
        in_specs=[hbm] * 2,
        out_specs=[hbm] * 2,
        scratch_shapes=[pltpu.SemaphoreType.DMA((2,))],
        compiler_params=pltpu.CompilerParams(vmem_limit_bytes=1024 * 1024),
        cost_estimate=pl.CostEstimate(
            flops=0, bytes_accessed=8 * half * BLK * BLK, transcendentals=0
        ),
        name="halves",
    )(up, down)


def pick_kernel(at_ref, blocks_ref, *outs):
    for n, out in enumerate(outs):
        for i in range(SEL):
            out[i] = blocks_ref[at_ref[n * SEL + i]]


def pick(blocks, at):
    n = len(OFFSETS)
    vmem = pl.BlockSpec(memory_space=pltpu.VMEM)
    return pl.pallas_call(
        pick_kernel,
        out_shape=[jax.ShapeDtypeStruct((SEL, BLK, BLK), jnp.bfloat16)] * n,
        in_specs=[pl.BlockSpec(memory_space=pltpu.SMEM), vmem],
        out_specs=[vmem] * n,
        compiler_params=pltpu.CompilerParams(vmem_limit_bytes=8 * 1024 * 1024),
        cost_estimate=pl.CostEstimate(
            flops=0, bytes_accessed=4 * n * SEL * BLK * BLK, transcendentals=0
        ),
        name="pick",
    )(at, blocks)


def products_kernel(n_panel, n_left, n_add, idx_ref, order_ref, count_ref, *refs):
    panel_refs, refs = refs[:n_panel], refs[n_panel:]
    left_refs, refs = refs[:n_left], refs[n_left:]
    add_refs, out_refs = refs[:n_add], refs[n_add:-4]
    panel, lefts, panel_sem, left_sem = refs[-4:]
    copies = []
    at = 0
    for n, ref in enumerate(panel_refs):
        size = ref.shape[0]
        copies.append(pltpu.make_async_copy(ref, panel.at[pl.ds(at, size)], panel_sem.at[n]))
        at += size
    for r, ref in enumerate(left_refs):
        copies.append(pltpu.make_async_copy(ref, lefts.at[r], left_sem.at[r]))
    for copy in copies:
        copy.start()
    panel[at] = jnp.zeros((BLK, BLK), panel.dtype)
    for copy in copies:
        copy.wait()
    for r in range(n_left):
        pairs_here = (count_ref[r] + 1) // 2
        for pairs in range(SEL // 2 + 1):

            @pl.when(pairs_here == pairs)
            def _(r=r, pairs=pairs):
                def step(sp, inner):
                    s0 = 2 * sp
                    if pairs:
                        strips = []
                        for t in range(2 * pairs):
                            spot = (r * SEL + t) * KEPT + s0
                            strips.append(
                                jnp.concatenate(
                                    [panel[idx_ref[spot]], panel[idx_ref[spot + 1]]], axis=1
                                )
                            )
                        lhs = jnp.concatenate(
                            [lefts[r, order_ref[r * SEL + t]] for t in range(2 * pairs)], axis=1
                        )
                        total = jnp.dot(
                            lhs,
                            jnp.concatenate(strips, axis=0),
                            preferred_element_type=jnp.float32,
                        )
                    else:
                        total = jnp.zeros((BLK, 2 * BLK), jnp.float32)
                    both = [total[:, :BLK], total[:, BLK:]]
                    for k in range(2):
                        if n_add:
                            both[k] = both[k] + add_refs[r][0, s0 + k].astype(jnp.float32)
                        out_refs[r][0, s0 + k] = both[k].astype(jnp.bfloat16)
                    return inner

                lax.fori_loop(0, KEPT // 2, step, 0, unroll=4)


def products(table, panel_parts, lefts, adds=()):
    n = len(lefts)
    total = sum(part.shape[0] for part in panel_parts)
    smem = pl.BlockSpec(memory_space=pltpu.SMEM)
    hbm = pl.BlockSpec(memory_space=pl.ANY)
    vmem = pl.BlockSpec(memory_space=pltpu.VMEM)
    return pl.pallas_call(
        functools.partial(products_kernel, len(panel_parts), n, len(adds)),
        out_shape=[jax.ShapeDtypeStruct((1, KEPT, BLK, BLK), jnp.bfloat16)] * n,
        in_specs=[smem] * 3 + [hbm] * (len(panel_parts) + n) + [vmem] * len(adds),
        out_specs=[vmem] * n,
        scratch_shapes=[
            pltpu.VMEM((total + 1, BLK, BLK), jnp.bfloat16),
            pltpu.VMEM((n, SEL, BLK, BLK), jnp.bfloat16),
            pltpu.SemaphoreType.DMA((len(panel_parts),)),
            pltpu.SemaphoreType.DMA((n,)),
        ],
        compiler_params=pltpu.CompilerParams(vmem_limit_bytes=24 * 1024 * 1024),
        cost_estimate=pl.CostEstimate(
            flops=n * KEPT * SEL * 2 * BLK**3,
            bytes_accessed=total * BLK * BLK * 2,
            transcendentals=0,
        ),
        name="products",
    )(*table, *panel_parts, *lefts, *adds)


def plus_kernel(rows, *refs):
    out_ref = refs[-1]

    def step(i, carry):
        total = refs[0][rows[0], i].astype(jnp.float32)
        for row, ref in zip(rows[1:], refs[1:-1]):
            total = total + ref[row, i].astype(jnp.float32)
        out_ref[0, i] = total.astype(out_ref.dtype)
        return carry

    lax.fori_loop(0, KEPT, step, 0, unroll=4)


def plus(*terms):
    vmem = pl.BlockSpec(memory_space=pltpu.VMEM)
    return pl.pallas_call(
        functools.partial(plus_kernel, tuple(row for _, row in terms)),
        out_shape=jax.ShapeDtypeStruct((1, KEPT, BLK, BLK), jnp.bfloat16),
        in_specs=[vmem] * len(terms),
        out_specs=vmem,
        compiler_params=pltpu.CompilerParams(vmem_limit_bytes=16 * 1024 * 1024),
        cost_estimate=pl.CostEstimate(
            flops=0, bytes_accessed=(len(terms) + 1) * KEPT * BLK * BLK * 2, transcendentals=0
        ),
        name="plus",
    )(*(array for array, _ in terms))


def stage(*arrays):
    return lax.optimization_barrier(arrays)


def reached(z):
    j = jnp.arange(SEL, dtype=jnp.int32)
    return (z + NZ // 2 * (j // ROWS)) % NZ * ROWS + j % ROWS


def local(left_blocks, left_cols, reach_blocks, reach_cols):
    z = lax.axis_index("row")
    col = lax.axis_index("col")
    c = col % NC
    x = col // NC % NX
    y = col // (NC * NX)
    sign = 1 - 2 * c
    blocks = reach_blocks[:, 0]

    own_left = left_blocks[0, 0]
    cols_here = left_cols[:, 0]
    own_cols = lax.dynamic_index_in_dim(cols_here, z, 0, keepdims=False)
    names = jnp.concatenate([reached(z + offset * sign + NZ) for offset in OFFSETS])
    picked_at = jnp.argmax(names[:, None] == own_cols[None, :], axis=1)

    def round_one(block):
        return [in_plane(block, distance, 0) for distance in (1, -1, 2)]

    picked_at, reach_cols = stage(picked_at.astype(jnp.int32), reach_cols)
    far_cols, near_ring, picked, far_set = stage(
        send(reach_cols, lambda z, y, x, c: (z + NZ // 2, y, x, c)),
        round_one(blocks),
        pick(own_left, picked_at),
        send(blocks, lambda z, y, x, c: (z + NZ // 2, y, x, c)),
    )
    far_l, near_l, leaf_l, own_l = picked
    far_l = along_z(far_l, 2)
    far_ring, leaf_l = stage(round_one(far_set), leaf_l)
    first = join((blocks, *near_ring), (far_set, *far_ring))

    steps = jnp.array(OFFSETS, dtype=jnp.int32)
    cols = cols_here[(z - steps * sign + NZ) % NZ]
    slot = jnp.arange(KEPT, dtype=jnp.int32)

    def place(offset):
        offset = offset % 4
        return jnp.where(offset == 0, 0, jnp.where(offset == 3, 1, jnp.where(offset == 1, 2, 3)))

    dx = place(slot // NC % NX - x + NX)
    dy = place(slot // (NC * NX) - y + NY)
    then, ahead = jnp.where(slot % NC == 0, dy, dx), jnp.where(slot % NC == 0, dx, dy)
    turn = jnp.where(slot % NC == c, jnp.where(then == 3, 6, then), jnp.where(then == 3, 7, then + 3))
    near_place = turn * 64 + ahead * 8
    j = jnp.arange(SEL, dtype=jnp.int32)

    kept = jnp.concatenate([reach_cols, far_cols], axis=0)
    place_of = near_place[None, :] + (j // ROWS * 32 + j % ROWS)[:, None]
    present = jnp.any(reached(z)[None, :, None] == cols[:, None, :], axis=2)
    rank = jnp.sum(present[:, None, :] & (j[None, None, :] < j[None, :, None]), axis=2)
    hit = present[:, None, :] & (rank[:, None, :] == j[None, :, None])
    order = jnp.sum(jnp.where(hit, j[None, None, :], 0), axis=2)
    same = kept[None, :, None, :] == cols[:, None, :, None]
    at = jnp.sum(jnp.where(same, place_of[None, :, None, :] - SET, 0), axis=3)
    idx = SET + jnp.sum(jnp.where(hit[:, :, :, None], at[:, None, :, :], 0), axis=2)
    count = jnp.sum(present.astype(jnp.int32), axis=1)
    idx_early = jnp.where(idx < EARLY, idx, EARLY)
    idx_late = jnp.where((idx >= EARLY) & (idx < SET), idx - EARLY, SET - EARLY)

    def entry(blocks_at, first, last):
        return tuple(t[first:last].reshape(-1) for t in (blocks_at, order, count))

    tables = entry(idx_early, 0, 1), entry(idx_late, 0, 1), entry(idx, 1, 3), entry(idx, 3, 4)

    tables, ready = stage(tables, first)
    tables, far_l, leaf_l, first_got, first, up, down, near_l = stage(
        tables,
        far_l,
        along_z(leaf_l, -1),
        swap(ready),
        first,
        in_plane(first, 1, 1),
        in_plane(first, -1, 1),
        near_l,
    )
    near_half, far_half = halves(up, down)
    up, down, near_l, near_half, far_half = stage(up, down, near_l, near_half, far_half)
    up_got, down_got = swap(up), swap(down)
    early = (first, up, down, first_got, up_got, down_got)
    up_got, down_got, near_l, near_on, far_on, early_term = stage(
        up_got,
        down_got,
        along_z(near_l, 1),
        in_plane(near_half, 1, 1),
        in_plane(far_half, -1, 1),
        products(tables[0], early, (far_l,)),
    )
    early = early[:4] + (up_got, down_got)
    late = (near_on, far_on, swap(near_on), swap(far_on))

    (far_term,) = products(tables[1], late, (far_l,), early_term)
    far_got = along_z(far_term, -1)
    near_l, leaf_l, far_term = stage(near_l, leaf_l, far_term)
    near_term, leaf_term = products(tables[2], early + late, (near_l, leaf_l))
    leaf_got = along_z(leaf_term, 1)
    near_got = along_z(plus((near_term, 0), (far_got, 0)), -1)
    own_l, leaf_term = stage(own_l, leaf_term)
    (own_term,) = products(tables[3], early + late, (own_l,))
    return plus((own_term, 0), (leaf_got, 0), (near_got, 0))[None]


def solution(mesh):
    in_specs = (
        P("row", "col", None, None, None),
        P(None, "col", None),
        P("row", "col", None, None),
        P("row", None),
    )
    out_specs = P("row", "col", None, None, None)
    return jax.shard_map(local, mesh=mesh, in_specs=in_specs, out_specs=out_specs, check_vma=False)
```

```python
import functools

import jax
import jax.numpy as jnp
from jax import lax
from jax.experimental import pallas as pl
from jax.experimental.pallas import tpu as pltpu
from jax.sharding import PartitionSpec as P

BLK = 128
NZ, NY, NX, NC = 8, 4, 4, 2
KEPT = 32
ROWS = 8
SEL = 16
SET = 512
EARLY = 384
AXES = ("row", "col")
OFFSETS = (2, 1, -1, 0)


def send(block, target):
    pairs = []
    for z in range(NZ):
        for y in range(NY):
            for x in range(NX):
                for c in range(NC):
                    tz, ty, tx, tc = target(z, y, x, c)
                    tz, ty, tx = tz % NZ, ty % NY, tx % NX
                    src = ((z * NY + y) * NX + x) * NC + c
                    dst = ((tz * NY + ty) * NX + tx) * NC + tc
                    pairs.append((src, dst))
    return lax.ppermute(block, AXES, pairs)


def swap(block):
    return send(block, lambda z, y, x, c: (z, y, x, 1 - c))


def along_z(block, distance):
    return send(block, lambda z, y, x, c: (z + distance * (1 - 2 * c), y, x, c))


def in_plane(block, distance, flip):
    def target(z, y, x, c):
        if c ^ flip:
            return (z, y + distance, x, c)
        return (z, y, x + distance, c)

    return send(block, target)


def join_kernel(*refs):
    parts, out_ref, sems = refs[:-2], refs[-2], refs[-1]
    copies = []
    at = 0
    for n, ref in enumerate(parts):
        size = ref.shape[0]
        copies.append(pltpu.make_async_copy(ref, out_ref.at[pl.ds(at, size)], sems.at[n]))
        at += size
    for copy in copies:
        copy.start()
    for copy in copies:
        copy.wait()


def join(parts, others):
    total = sum(part.shape[0] for part in parts + others)
    return pl.pallas_call(
        join_kernel,
        out_shape=jax.ShapeDtypeStruct((total, BLK, BLK), jnp.bfloat16),
        in_specs=[pl.BlockSpec(memory_space=pltpu.HBM)] * len(parts)
        + [pl.BlockSpec(memory_space=pl.ANY)] * len(others),
        out_specs=pl.BlockSpec(memory_space=pltpu.VMEM),
        scratch_shapes=[pltpu.SemaphoreType.DMA((len(parts + others),))],
        compiler_params=pltpu.CompilerParams(vmem_limit_bytes=4 * 1024 * 1024),
        cost_estimate=pl.CostEstimate(
            flops=0, bytes_accessed=4 * total * BLK * BLK, transcendentals=0
        ),
        name="join",
    )(*(pltpu.with_memory_space_constraint(part, pltpu.HBM) for part in parts), *others)


def halves_kernel(up_ref, down_ref, first_ref, second_ref, sems):
    half = first_ref.shape[0]
    copies = [
        pltpu.make_async_copy(up_ref.at[pl.ds(0, half)], first_ref, sems.at[0]),
        pltpu.make_async_copy(down_ref.at[pl.ds(half, half)], second_ref, sems.at[1]),
    ]
    for copy in copies:
        copy.start()
    for copy in copies:
        copy.wait()


def halves(up, down):
    half = up.shape[0] // 2
    hbm = pl.BlockSpec(memory_space=pl.ANY)
    return pl.pallas_call(
        halves_kernel,
        out_shape=[jax.ShapeDtypeStruct((half, BLK, BLK), jnp.bfloat16)] * 2,
        in_specs=[hbm] * 2,
        out_specs=[hbm] * 2,
        scratch_shapes=[pltpu.SemaphoreType.DMA((2,))],
        compiler_params=pltpu.CompilerParams(vmem_limit_bytes=1024 * 1024),
        cost_estimate=pl.CostEstimate(
            flops=0, bytes_accessed=8 * half * BLK * BLK, transcendentals=0
        ),
        name="halves",
    )(up, down)


def pick_kernel(at_ref, blocks_ref, *outs):
    for n, out in enumerate(outs):
        for i in range(SEL):
            out[i] = blocks_ref[at_ref[n * SEL + i]]


def pick(blocks, at):
    n = len(OFFSETS)
    vmem = pl.BlockSpec(memory_space=pltpu.VMEM)
    return pl.pallas_call(
        pick_kernel,
        out_shape=[jax.ShapeDtypeStruct((SEL, BLK, BLK), jnp.bfloat16)] * n,
        in_specs=[pl.BlockSpec(memory_space=pltpu.SMEM), vmem],
        out_specs=[vmem] * n,
        compiler_params=pltpu.CompilerParams(vmem_limit_bytes=8 * 1024 * 1024),
        cost_estimate=pl.CostEstimate(
            flops=0, bytes_accessed=4 * n * SEL * BLK * BLK, transcendentals=0
        ),
        name="pick",
    )(at, blocks)


def products_kernel(n_panel, n_left, n_add, idx_ref, order_ref, count_ref, *refs):
    panel_refs, refs = refs[:n_panel], refs[n_panel:]
    left_refs, refs = refs[:n_left], refs[n_left:]
    add_refs, out_refs = refs[:n_add], refs[n_add:-4]
    panel, lefts, panel_sem, left_sem = refs[-4:]
    copies = []
    at = 0
    for n, ref in enumerate(panel_refs):
        size = ref.shape[0]
        copies.append(pltpu.make_async_copy(ref, panel.at[pl.ds(at, size)], panel_sem.at[n]))
        at += size
    for r, ref in enumerate(left_refs):
        copies.append(pltpu.make_async_copy(ref, lefts.at[r], left_sem.at[r]))
    for copy in copies:
        copy.start()
    panel[at] = jnp.zeros((BLK, BLK), panel.dtype)
    for copy in copies:
        copy.wait()
    for r in range(n_left):
        pairs_here = (count_ref[r] + 1) // 2
        for pairs in range(SEL // 2 + 1):

            @pl.when(pairs_here == pairs)
            def _(r=r, pairs=pairs):
                def step(sp, inner):
                    s0 = 2 * sp
                    if pairs:
                        strips = []
                        for t in range(2 * pairs):
                            spot = (r * SEL + t) * KEPT + s0
                            strips.append(
                                jnp.concatenate(
                                    [panel[idx_ref[spot]], panel[idx_ref[spot + 1]]], axis=1
                                )
                            )
                        lhs = jnp.concatenate(
                            [lefts[r, order_ref[r * SEL + t]] for t in range(2 * pairs)], axis=1
                        )
                        total = jnp.dot(
                            lhs,
                            jnp.concatenate(strips, axis=0),
                            preferred_element_type=jnp.float32,
                        )
                    else:
                        total = jnp.zeros((BLK, 2 * BLK), jnp.float32)
                    both = [total[:, :BLK], total[:, BLK:]]
                    for k in range(2):
                        if n_add:
                            both[k] = both[k] + add_refs[r][0, s0 + k].astype(jnp.float32)
                        out_refs[r][0, s0 + k] = both[k].astype(jnp.bfloat16)
                    return inner

                lax.fori_loop(0, KEPT // 2, step, 0, unroll=4)


def products(table, panel_parts, lefts, adds=()):
    n = len(lefts)
    total = sum(part.shape[0] for part in panel_parts)
    smem = pl.BlockSpec(memory_space=pltpu.SMEM)
    hbm = pl.BlockSpec(memory_space=pl.ANY)
    vmem = pl.BlockSpec(memory_space=pltpu.VMEM)
    return pl.pallas_call(
        functools.partial(products_kernel, len(panel_parts), n, len(adds)),
        out_shape=[jax.ShapeDtypeStruct((1, KEPT, BLK, BLK), jnp.bfloat16)] * n,
        in_specs=[smem] * 3 + [hbm] * (len(panel_parts) + n) + [vmem] * len(adds),
        out_specs=[vmem] * n,
        scratch_shapes=[
            pltpu.VMEM((total + 1, BLK, BLK), jnp.bfloat16),
            pltpu.VMEM((n, SEL, BLK, BLK), jnp.bfloat16),
            pltpu.SemaphoreType.DMA((len(panel_parts),)),
            pltpu.SemaphoreType.DMA((n,)),
        ],
        compiler_params=pltpu.CompilerParams(vmem_limit_bytes=24 * 1024 * 1024),
        cost_estimate=pl.CostEstimate(
            flops=n * KEPT * SEL * 2 * BLK**3,
            bytes_accessed=total * BLK * BLK * 2,
            transcendentals=0,
        ),
        name="products",
    )(*table, *panel_parts, *lefts, *adds)


def plus_kernel(rows, *refs):
    out_ref = refs[-1]

    def step(i, carry):
        total = refs[0][rows[0], i].astype(jnp.float32)
        for row, ref in zip(rows[1:], refs[1:-1]):
            total = total + ref[row, i].astype(jnp.float32)
        out_ref[0, i] = total.astype(out_ref.dtype)
        return carry

    lax.fori_loop(0, KEPT, step, 0, unroll=4)


def plus(*terms):
    vmem = pl.BlockSpec(memory_space=pltpu.VMEM)
    return pl.pallas_call(
        functools.partial(plus_kernel, tuple(row for _, row in terms)),
        out_shape=jax.ShapeDtypeStruct((1, KEPT, BLK, BLK), jnp.bfloat16),
        in_specs=[vmem] * len(terms),
        out_specs=vmem,
        compiler_params=pltpu.CompilerParams(vmem_limit_bytes=16 * 1024 * 1024),
        cost_estimate=pl.CostEstimate(
            flops=0, bytes_accessed=(len(terms) + 1) * KEPT * BLK * BLK * 2, transcendentals=0
        ),
        name="plus",
    )(*(array for array, _ in terms))


def stage(*arrays):
    return lax.optimization_barrier(arrays)


def reached(z):
    j = jnp.arange(SEL, dtype=jnp.int32)
    return (z + NZ // 2 * (j // ROWS)) % NZ * ROWS + j % ROWS


def local(left_blocks, left_cols, reach_blocks, reach_cols):
    z = lax.axis_index("row")
    col = lax.axis_index("col")
    c = col % NC
    x = col // NC % NX
    y = col // (NC * NX)
    sign = 1 - 2 * c
    blocks = reach_blocks[:, 0]

    own_left = left_blocks[0, 0]
    cols_here = left_cols[:, 0]
    own_cols = lax.dynamic_index_in_dim(cols_here, z, 0, keepdims=False)
    names = jnp.concatenate([reached(z + offset * sign + NZ) for offset in OFFSETS])
    picked_at = jnp.argmax(names[:, None] == own_cols[None, :], axis=1)

    def round_one(block):
        return [in_plane(block, distance, 0) for distance in (1, -1, 2)]

    picked_at, reach_cols = stage(picked_at.astype(jnp.int32), reach_cols)
    far_cols, near_ring, picked, far_set = stage(
        send(reach_cols, lambda z, y, x, c: (z + NZ // 2, y, x, c)),
        round_one(blocks),
        pick(own_left, picked_at),
        send(blocks, lambda z, y, x, c: (z + NZ // 2, y, x, c)),
    )
    far_l, near_l, leaf_l, own_l = picked
    far_l = along_z(far_l, 2)
    steps = jnp.array(OFFSETS, dtype=jnp.int32)
    cols = cols_here[(z - steps * sign + NZ) % NZ]
    slot = jnp.arange(KEPT, dtype=jnp.int32)

    def place(offset):
        offset = offset % 4
        return jnp.where(offset == 0, 0, jnp.where(offset == 3, 1, jnp.where(offset == 1, 2, 3)))

    dx = place(slot // NC % NX - x + NX)
    dy = place(slot // (NC * NX) - y + NY)
    then, ahead = jnp.where(slot % NC == 0, dy, dx), jnp.where(slot % NC == 0, dx, dy)
    turn = jnp.where(slot % NC == c, jnp.where(then == 3, 6, then), jnp.where(then == 3, 7, then + 3))
    near_place = turn * 64 + ahead * 8
    j = jnp.arange(SEL, dtype=jnp.int32)

    kept = jnp.concatenate([reach_cols, far_cols], axis=0)
    place_of = near_place[None, :] + (j // ROWS * 32 + j % ROWS)[:, None]
    present = jnp.any(reached(z)[None, :, None] == cols[:, None, :], axis=2)
    rank = jnp.sum(present[:, None, :] & (j[None, None, :] < j[None, :, None]), axis=2)
    hit = present[:, None, :] & (rank[:, None, :] == j[None, :, None])
    order = jnp.sum(jnp.where(hit, j[None, None, :], 0), axis=2)
    same = kept[None, :, None, :] == cols[:, None, :, None]
    at = jnp.sum(jnp.where(same, place_of[None, :, None, :] - SET, 0), axis=3)
    idx = SET + jnp.sum(jnp.where(hit[:, :, :, None], at[:, None, :, :], 0), axis=2)
    count = jnp.sum(present.astype(jnp.int32), axis=1)
    idx_early = jnp.where(idx < EARLY, idx, EARLY)
    idx_late = jnp.where((idx >= EARLY) & (idx < SET), idx - EARLY, SET - EARLY)

    def entry(blocks_at, first, last):
        return tuple(t[first:last].reshape(-1) for t in (blocks_at, order, count))

    tables = entry(idx_early, 0, 1), entry(idx_late, 0, 1), entry(idx, 1, 3), entry(idx, 3, 4)

    far_ring, leaf_l, tables = stage(round_one(far_set), leaf_l, tables)
    first = join((blocks, *near_ring), (far_set, *far_ring))
    tables, far_l, leaf_l, first_got, first, up, down, near_l = stage(
        tables,
        far_l,
        along_z(leaf_l, -1),
        swap(first),
        first,
        in_plane(first, 1, 1),
        in_plane(first, -1, 1),
        near_l,
    )
    near_half, far_half = halves(up, down)
    up, down, near_l, near_half, far_half = stage(up, down, near_l, near_half, far_half)
    up_got, down_got = swap(up), swap(down)
    early = (first, up, down, first_got, up_got, down_got)
    up_got, down_got, near_l, near_on, far_on, early_term = stage(
        up_got,
        down_got,
        along_z(near_l, 1),
        in_plane(near_half, 1, 1),
        in_plane(far_half, -1, 1),
        products(tables[0], early, (far_l,)),
    )
    early = early[:4] + (up_got, down_got)
    late = (near_on, far_on, swap(near_on), swap(far_on))

    (far_term,) = products(tables[1], late, (far_l,), early_term)
    far_got = along_z(far_term, -1)
    near_l, leaf_l, far_term = stage(near_l, leaf_l, far_term)
    near_term, leaf_term = products(tables[2], early + late, (near_l, leaf_l))
    leaf_got = along_z(leaf_term, 1)
    near_got = along_z(plus((near_term, 0), (far_got, 0)), -1)
    own_l, leaf_term = stage(own_l, leaf_term)
    (own_term,) = products(tables[3], early + late, (own_l,))
    return plus((own_term, 0), (leaf_got, 0), (near_got, 0))[None]


def solution(mesh):
    in_specs = (
        P("row", "col", None, None, None),
        P(None, "col", None),
        P("row", "col", None, None),
        P("row", None),
    )
    out_specs = P("row", "col", None, None, None)
    return jax.shard_map(local, mesh=mesh, in_specs=in_specs, out_specs=out_specs, check_vma=False)
```
